32 devices in a mesh: dom: 2 (over y), grp: 4 (over x, core), tp: 4 (over z).
Axes of the slice: x: 2, y: 2, z: 4, core: 2. Of those that a mesh axis runs over, the one named last changes fastest.
Arguments:
- acts: bfloat16 [4096, 8192], P(('dom', 'grp'), 'tp'), parts along dimension 0, may hold values from -6 to 6
- output_weight_matrix: bfloat16 [8192, 8192], P(None, 'tp'), may hold values from -0.0625 to 0.0625
- adapter_down_factors: bfloat16 [32, 8192, 64], P('grp', 'tp'), may hold values from -0.0625 to 0.0625
- adapter_up_factors: bfloat16 [32, 64, 8192], P('grp', None, 'tp'), may hold values from -0.75 to 0.75
- adapter_pairings: int32 [8, 4, 2], P('dom'), parts along dimension 0, may hold values from 0 to 7, as said below
- request_working_slot: int32 [4096], P(('dom', 'grp')), parts along dimension 0, may hold values from 0 to 7
Outputs:
- projected_out: bfloat16 [4096, 8192], P(('dom', 'grp'), 'tp'), parts along dimension 0
The draws below stay inside these ranges and needn't reach their ends.
There are 2 independent parts, one for each index of `dom`. The reference program is written for one: setup_inputs(seed, part) draws one part's arguments, and reference() takes and returns one part's arrays. A program takes and returns all parts, laid end to end along the dimension named above; an argument that names none is the same for every part. Nothing has to cross between parts.
Inputs may be any that keep to these rules, and one draw needn't show every extreme that they name: The 2 entries adapter_pairings[s, d, :] of one pair differ.
All inputs are finite; a program needn't handle non-finite values.
Results may differ from the reference program's by a relative error of at most 0.0041.
Values may be sent and summed in bfloat16 or wider, within the bound.
A program may use at most 192 MiB of HBM per device.

```python
import jax
import jax.numpy as jnp
from jax import lax

MODEL_WIDTH = 8192
ADAPTER_RANK = 64
REQ_GRP = 512
ADP_GRP = 8
SLOTS = 2
GROUPS = 4
WORKING = 8
REQUESTS = 2048
ADAPTER_TOTAL = 32


def draw_adapter_pairings(key, part):
    key = jax.random.fold_in(key, 11)
    pair_count = GROUPS * GROUPS
    keys = jax.random.split(key, pair_count + 1)
    orders = jax.vmap(lambda inner: jax.random.permutation(inner, ADP_GRP))(keys[:pair_count])[:, :SLOTS]
    special = jax.random.randint(keys[pair_count], (), 0, pair_count)
    highest = (ADP_GRP - 1 - jnp.arange(SLOTS)).astype(jnp.int32)
    picked = jnp.where((jnp.arange(pair_count) == special)[:, None], highest[None, :], orders.astype(jnp.int32))
    return picked.reshape(GROUPS, GROUPS, SLOTS).astype(jnp.int32)


def draw_request_working_slot(key, part):
    key = jax.random.fold_in(key, 23)
    first, second = jax.random.split(key)
    slot_ids = jax.random.randint(first, (REQUESTS,), 0, WORKING).astype(jnp.int32)
    places = jax.random.permutation(second, REQUESTS)
    slot_ids = slot_ids.at[places[0]].set(WORKING - 1)
    slot_ids = slot_ids.at[places[1]].set(0)
    return slot_ids.astype(jnp.int32)


def block_levels(key, shape, cuts, smallest, largest):
    factor_of = 1.0
    for position, blocks in cuts:
        steps = jax.random.uniform(jax.random.fold_in(jax.random.fold_in(key, 6), position), (blocks,), jnp.float32, smallest / len(cuts), largest / len(cuts))
        factor_of = factor_of * jnp.repeat(jnp.exp(steps), shape[position] // blocks).reshape((-1,) + (1,) * (len(shape) - 1 - position))
    return factor_of


def scatter_about(rng, shape, width, reach, cuts=(), kind=jnp.bfloat16):
    array = jax.random.normal(rng, shape, jnp.float32) * width
    if len(cuts) > 0:
        array = block_levels(rng, shape, cuts, -0.22, 0.18) * array
    return jnp.clip(array, min=-reach, max=reach).astype(kind)


def setup_inputs(seed: int = 0, part: int = 0) -> dict:
    key_of = jax.random.split(jax.random.key(seed), 7)
    part_splits = jax.random.split(jax.random.fold_in(key_of[6], part), 7)
    return {
        "acts": scatter_about(part_splits[0], (REQUESTS, MODEL_WIDTH), 1.0, 6.0, ((0, 4), (1, 4))),
        "output_weight_matrix": scatter_about(key_of[1], (MODEL_WIDTH, MODEL_WIDTH), MODEL_WIDTH ** -0.5, 0.0625, ((1, 4),)),
        "adapter_down_factors": scatter_about(key_of[2], (ADAPTER_TOTAL, MODEL_WIDTH, ADAPTER_RANK), MODEL_WIDTH ** -0.5, 0.0625, ((0, 4), (1, 4))),
        "adapter_up_factors": scatter_about(key_of[3], (ADAPTER_TOTAL, ADAPTER_RANK, MODEL_WIDTH), ADAPTER_RANK ** -0.5, 0.75, ((0, 4), (2, 4))),
        "adapter_pairings": draw_adapter_pairings(jax.random.fold_in(jax.random.fold_in(key_of[6], part), 71), part),
        "request_working_slot": draw_request_working_slot(jax.random.fold_in(jax.random.fold_in(key_of[6], part), 71), part),
    }


def reference(acts, output_weight_matrix, adapter_down_factors, adapter_up_factors, adapter_pairings, request_working_slot):
    def one_group(group):
        rows_x = lax.dynamic_slice_in_dim(acts, group * REQ_GRP, REQ_GRP, 0)
        wanted = lax.dynamic_slice_in_dim(request_working_slot, group * REQ_GRP, REQ_GRP, 0)
        column = jnp.take(adapter_pairings, group, axis=1)
        selected_adapter = (jnp.arange(GROUPS, dtype=jnp.int32)[:, None] * ADP_GRP + column).reshape(-1).astype(jnp.int32)
        down_factor_rows = jnp.take(adapter_down_factors, selected_adapter, axis=0).astype(jnp.float32)
        up_factor_rows = jnp.take(adapter_up_factors, selected_adapter, axis=0)
        onehot = wanted[:, None] == jnp.arange(WORKING, dtype=jnp.int32)[None, :]
        scores = jnp.einsum("rd,wdk->rwk", rows_x.astype(jnp.float32), down_factor_rows)
        rank_sum = jnp.sum(jnp.where(onehot[:, :, None], scores, jnp.float32(0.0)), axis=1)
        rank_bf = rank_sum.astype(jnp.bfloat16)
        spread = jnp.where(onehot[:, :, None], rank_bf[:, None, :], jnp.zeros((), jnp.bfloat16))
        spread = spread.reshape(REQ_GRP, WORKING * ADAPTER_RANK)
        adapter_out = jnp.dot(spread, up_factor_rows.reshape(WORKING * ADAPTER_RANK, MODEL_WIDTH), preferred_element_type=jnp.float32)
        projected = jnp.dot(rows_x, output_weight_matrix, preferred_element_type=jnp.float32)
        return (projected + adapter_out).astype(jnp.bfloat16)

    result = lax.map(one_group, jnp.arange(GROUPS, dtype=jnp.int32))
    return result.reshape(REQUESTS, MODEL_WIDTH)
```

```python
import functools

import jax
import jax.numpy as jnp
from jax import lax
from jax.experimental import pallas as pl
from jax.experimental.pallas import tpu as pltpu
from jax.sharding import PartitionSpec as P

MESH = pl.DeviceIdType.MESH


def divisor(size, most):
    return most if size % most == 0 else size


def kernel(
    tp, groups, chunks,
    acts, weight, down, up, pairings, slots, out,
    gathered, weights, acc, down_local, up_local, down_stage, up_stage, down_work, up_work,
    own_rank, low_in, low_out, high_in, high_out, staged,
    up_send, up_recv, dn_send, dn_recv, fac_send, fac_recv, rank_send, rank_recv,
    weight_sem, local_sem, out_sem,
):
    g, t = lax.axis_index("grp"), lax.axis_index("tp")
    batch, depth = acts.shape
    columns = weight.shape[1]
    rank = down.shape[2]
    rows = batch // chunks
    pair = pairings.shape[2]
    lanes = pair * rank
    half = batch // 2
    down_piece = down_local.shape[1]
    up_piece = up_local.shape[2]

    def row_block(c):
        return pl.ds(pl.multiple_of(c * rows, rows), rows)

    def peer(k):
        return lax.rem(g + k, groups)

    def weight_copy(j):
        return pltpu.make_async_copy(
            weight.at[pl.ds(pl.multiple_of(j * depth, depth), depth), :], weights.at[j], weight_sem.at[j]
        )

    own_copy = pltpu.make_async_copy(acts, gathered.at[t], local_sem.at[0])
    own_copy.start()

    barrier = pltpu.get_barrier_semaphore()

    @pl.when(t > 0)
    def _():
        pl.semaphore_signal(barrier, inc=1, device_id={"tp": t - 1}, device_id_type=MESH)

    @pl.when(t < tp - 1)
    def _():
        pl.semaphore_signal(barrier, inc=1, device_id={"tp": t + 1}, device_id_type=MESH)

    for k in range(1, groups):
        pl.semaphore_signal(barrier, inc=1, device_id={"grp": peer(k)}, device_id_type=MESH)
    pl.semaphore_wait(
        barrier, groups - 1 + jnp.where(t > 0, 1, 0) + jnp.where(t < tp - 1, 1, 0)
    )

    def own_send(c, to, send, recv):
        return pltpu.make_async_remote_copy(
            src_ref=acts.at[row_block(c), :], dst_ref=gathered.at[t, row_block(c), :],
            send_sem=send.at[0, c], recv_sem=recv.at[0, c],
            device_id={"tp": to}, device_id_type=MESH,
        )

    def passed(j, s, c, to, send, recv):
        return pltpu.make_async_remote_copy(
            src_ref=gathered.at[j, row_block(c), :], dst_ref=gathered.at[j, row_block(c), :],
            send_sem=send.at[s, c], recv_sem=recv.at[s, c],
            device_id={"tp": to}, device_id_type=MESH,
        )

    @pl.loop(0, chunks)
    def _(c):
        @pl.when(t > 0)
        def _():
            own_send(c, t - 1, dn_send, dn_recv).start()

        @pl.when(t < tp - 1)
        def _():
            own_send(c, t + 1, up_send, up_recv).start()

    def factor_send(which, k):
        stage, work = (down_stage, down_work) if which == 0 else (up_stage, up_work)
        return pltpu.make_async_remote_copy(
            src_ref=stage.at[peer(k)], dst_ref=work.at[g],
            send_sem=fac_send.at[which, k - 1], recv_sem=fac_recv.at[which, k - 1],
            device_id={"grp": peer(k)}, device_id_type=MESH,
        )

    def factor_own(which):
        stage, work = (down_stage, down_work) if which == 0 else (up_stage, up_work)
        return pltpu.make_async_copy(stage.at[g], work.at[g], local_sem.at[2])

    @pl.loop(0, depth // down_piece)
    def _(p):
        span = pl.ds(pl.multiple_of(p * down_piece, down_piece), down_piece)
        load = pltpu.make_async_copy(down.at[:, span, :], down_local, local_sem.at[1])
        load.start()
        load.wait()

        @pl.loop(0, groups)
        def _(d):
            down_stage[d, span, :] = jnp.concatenate(
                [down_local[pairings[g, d, k]] for k in range(pair)], axis=1
            )

    for k in range(1, groups):
        factor_send(0, k).start()
    factor_own(0).start()
    factor_own(0).wait()

    @pl.loop(0, columns // up_piece)
    def _(p):
        span = pl.ds(pl.multiple_of(p * up_piece, up_piece), up_piece)
        load = pltpu.make_async_copy(up.at[:, :, span], up_local, local_sem.at[1])
        load.start()
        load.wait()

        @pl.loop(0, groups)
        def _(d):
            for k in range(pair):
                up_stage[d, k * rank:(k + 1) * rank, span] = up_local[pairings[g, d, k]]

    for k in range(1, groups):
        factor_send(1, k).start()
    factor_own(1).start()
    factor_own(1).wait()

    @pl.loop(0, tp)
    def _(j):
        weight_copy(j).start()

    own_copy.wait()

    @pl.loop(0, tp)
    def _(j):
        weight_copy(j).wait()

    tile = divisor(columns, 512)

    def product(j, c, first):
        @pl.loop(0, columns // tile)
        def _(n):
            span = pl.ds(pl.multiple_of(n * tile, tile), tile)
            part = jnp.dot(
                gathered[j, row_block(c), :], weights[j, :, span], preferred_element_type=jnp.float32
            )
            if first:
                acc[row_block(c), span] = part
            else:
                acc[row_block(c), span] += part

    @pl.loop(0, chunks)
    def _(c):
        product(t, c, True)

    for k in range(1, groups):
        factor_send(0, k).wait_recv()
    lane = lax.broadcasted_iota(jnp.int32, (batch, lanes), 1)
    lane_pair = lane // rank

    def one_group(s, total):
        scores = jnp.dot(gathered[t], down_work[s], preferred_element_type=jnp.float32)
        return total + jnp.where(slots[...] == s * pair + lane_pair, scores, 0.0)

    chosen = lax.fori_loop(0, groups, one_group, jnp.zeros((batch, lanes), jnp.float32))
    folded = chosen + pltpu.roll(chosen, rank, 1)
    low_lane = lax.broadcasted_iota(jnp.int32, (half, lanes), 1) < rank
    own_rank[...] = jnp.where(low_lane, folded[:half], folded[half:])

    def rank_pass(way, to):
        source, target = (low_out, low_in) if way == 0 else (high_out, high_in)
        return pltpu.make_async_remote_copy(
            src_ref=source, dst_ref=target,
            send_sem=rank_send.at[way], recv_sem=rank_recv.at[way],
            device_id={"tp": to}, device_id_type=MESH,
        )

    @pl.when(t == 0)
    def _():
        low_out[...] = own_rank[...]
        rank_pass(0, t + 1).start()

    @pl.when(t == tp - 1)
    def _():
        high_out[...] = own_rank[...]
        rank_pass(1, t - 1).start()

    def rank_hop(s):
        @pl.when(t == s)
        def _():
            rank_pass(0, t).wait_recv()

            @pl.when(t < tp - 1)
            def _():
                low_out[...] = low_in[...] + own_rank[...]
                rank_pass(0, t + 1).start()

        @pl.when(t == tp - 1 - s)
        def _():
            rank_pass(1, t).wait_recv()

            @pl.when(t > 0)
            def _():
                high_out[...] = high_in[...] + own_rank[...]
                rank_pass(1, t - 1).start()

    def add_adapters():
        @pl.when(t > 0)
        def _():
            own_rank[...] += low_in[...]

        @pl.when(t < tp - 1)
        def _():
            own_rank[...] += high_in[...]

        packed = own_rank[...]
        turned = pltpu.roll(packed, rank, 1)
        sums = jnp.concatenate(
            [jnp.where(low_lane, packed, turned), jnp.where(low_lane, turned, packed)], axis=0
        )
        for k in range(1, groups):
            factor_send(1, k).wait_recv()

        @pl.loop(0, groups)
        def _(s):
            spread = jnp.where(slots[...] == s * pair + lane_pair, sums, 0.0).astype(jnp.bfloat16)

            @pl.loop(0, columns // tile)
            def _(n):
                span = pl.ds(pl.multiple_of(n * tile, tile), tile)
                acc[:, span] += jnp.dot(
                    spread, up_work[s, :, span], preferred_element_type=jnp.float32
                )

    def out_copy(c):
        return pltpu.make_async_copy(
            staged.at[row_block(c), :], out.at[row_block(c), :], out_sem.at[c]
        )

    @pl.loop(1, tp)
    def _(s):
        @pl.loop(0, chunks)
        def _(c):
            @pl.when(t >= s)
            def _():
                passed(t - s, s - 1, c, t, up_send, up_recv).wait_recv()

                @pl.when(t < tp - 1)
                def _():
                    passed(t - s, s, c, t + 1, up_send, up_recv).start()

            @pl.when(t + s < tp)
            def _():
                passed(t + s, s - 1, c, t, dn_send, dn_recv).wait_recv()

                @pl.when(t > 0)
                def _():
                    passed(t + s, s, c, t - 1, dn_send, dn_recv).start()

            @pl.when(c == 0)
            def _():
                rank_hop(s)

                @pl.when(s == tp - 1)
                def _():
                    add_adapters()

            @pl.when(t >= s)
            def _():
                product(t - s, c, False)

            @pl.when(t + s < tp)
            def _():
                product(t + s, c, False)

            @pl.when(s == tp - 1)
            def _():
                staged[row_block(c), :] = acc[row_block(c), :].astype(staged.dtype)
                out_copy(c).start()

    @pl.loop(0, tp)
    def _(s):
        @pl.loop(0, chunks)
        def _(c):
            @pl.when((t >= s) & (t < tp - 1))
            def _():
                passed(t, s, c, t, up_send, up_recv).wait_send()

            @pl.when((t + s < tp) & (t > 0))
            def _():
                passed(t, s, c, t, dn_send, dn_recv).wait_send()

    @pl.when(t < tp - 1)
    def _():
        rank_pass(0, t).wait_send()

    @pl.when(t > 0)
    def _():
        rank_pass(1, t).wait_send()

    for which in range(2):
        for k in range(1, groups):
            factor_send(which, k).wait_send()

    @pl.loop(0, chunks)
    def _(c):
        out_copy(c).wait()


def body(tp, groups, acts, weight, down, up, pairings, slots):
    batch, depth = acts.shape
    columns = weight.shape[1]
    held, _, rank = down.shape
    lanes = pairings.shape[2] * rank
    chunks = 4 if tp <= 8 else 1
    down_piece, up_piece = divisor(depth, 512), divisor(columns, 512)
    bf16, f32 = jnp.bfloat16, jnp.float32
    slot_lanes = jnp.broadcast_to(slots[:, None], (batch, lanes))
    anywhere = pl.BlockSpec(memory_space=pl.ANY)
    flops = 2 * batch * columns * depth * tp + 2 * batch * groups * lanes * (depth + columns)
    packed = pltpu.VMEM((batch // 2, lanes), f32)
    return pl.pallas_call(
        functools.partial(kernel, tp, groups, chunks),
        out_shape=jax.ShapeDtypeStruct((batch, columns), bf16),
        in_specs=[anywhere] * 4
        + [pl.BlockSpec(memory_space=pltpu.SMEM), pl.BlockSpec(memory_space=pltpu.VMEM)],
        out_specs=anywhere,
        scratch_shapes=[
            pltpu.VMEM((tp, batch, depth), bf16),
            pltpu.VMEM((tp, depth, columns), bf16),
            pltpu.VMEM((batch, columns), f32),
            pltpu.VMEM((held, down_piece, rank), bf16),
            pltpu.VMEM((held, rank, up_piece), bf16),
            pltpu.VMEM((groups, depth, lanes), bf16),
            pltpu.VMEM((groups, lanes, columns), bf16),
            pltpu.VMEM((groups, depth, lanes), bf16),
            pltpu.VMEM((groups, lanes, columns), bf16),
            packed, packed, packed, packed, packed,
            pltpu.VMEM((batch, columns), bf16),
            pltpu.SemaphoreType.DMA((tp, chunks)),
            pltpu.SemaphoreType.DMA((tp, chunks)),
            pltpu.SemaphoreType.DMA((tp, chunks)),
            pltpu.SemaphoreType.DMA((tp, chunks)),
            pltpu.SemaphoreType.DMA((2, groups)),
            pltpu.SemaphoreType.DMA((2, groups)),
            pltpu.SemaphoreType.DMA((2,)),
            pltpu.SemaphoreType.DMA((2,)),
            pltpu.SemaphoreType.DMA((tp,)),
            pltpu.SemaphoreType.DMA((3,)),
            pltpu.SemaphoreType.DMA((chunks,)),
        ],
        compiler_params=pltpu.CompilerParams(
            collective_id=0, has_side_effects=True, vmem_limit_bytes=62 << 20
        ),
        cost_estimate=pl.CostEstimate(
            flops=flops, bytes_accessed=2 * (weight.size + 3 * acts.size), transcendentals=0
        ),
    )(acts, weight, down, up, pairings, slot_lanes)


def solution(mesh):
    placed = (
        P(("dom", "grp"), "tp"),
        P(None, "tp"),
        P("grp", "tp", None),
        P("grp", None, "tp"),
        P("dom", None, None),
        P(("dom", "grp")),
    )
    return jax.shard_map(
        functools.partial(body, mesh.shape["tp"], mesh.shape["grp"]),
        mesh=mesh, in_specs=placed, out_specs=P(("dom", "grp"), "tp"), check_vma=False,
    )
```

```python
import functools

import jax
import jax.numpy as jnp
from jax import lax
from jax.experimental import pallas as pl
from jax.experimental.pallas import tpu as pltpu
from jax.sharding import PartitionSpec as P

MESH = pl.DeviceIdType.MESH


def divisor(size, most):
    return most if size % most == 0 else size


def kernel(
    tp, groups, chunks,
    acts, weight, down, up, pairings, slots, out,
    gathered, weights, acc, down_local, up_local, down_stage, up_stage, down_work, up_work,
    own_rank, low_in, low_out, high_in, high_out, sum_in, sum_out, slot_lanes, staged,
    up_send, up_recv, dn_send, dn_recv, fac_send, fac_recv, rank_send, rank_recv,
    weight_sem, own_sem, local_sem, out_sem,
):
    g, t = lax.axis_index("grp"), lax.axis_index("tp")
    batch, depth = acts.shape
    columns = weight.shape[1]
    rank = down.shape[1]
    part = depth // chunks
    pair = pairings.shape[1]
    lanes = pair * rank
    half = batch // 2

    def features(c):
        return pl.ds(pl.multiple_of(c * part, part), part)

    def peer(k):
        return lax.rem(g + k, groups)

    def weight_copy(j):
        return pltpu.make_async_copy(
            weight.at[pl.ds(pl.multiple_of(j * depth, depth), depth), :], weights.at[j], weight_sem.at[j]
        )

    def own_copy(c):
        return pltpu.make_async_copy(acts.at[:, features(c)], gathered.at[t * chunks + c], own_sem.at[c])

    barrier = pltpu.get_barrier_semaphore()

    @pl.when(t > 0)
    def _():
        pl.semaphore_signal(barrier, inc=1, device_id={"tp": t - 1}, device_id_type=MESH)

    @pl.when(t < tp - 1)
    def _():
        pl.semaphore_signal(barrier, inc=1, device_id={"tp": t + 1}, device_id_type=MESH)

    for k in range(1, groups):
        pl.semaphore_signal(barrier, inc=1, device_id={"grp": peer(k)}, device_id_type=MESH)
    pl.semaphore_wait(
        barrier, groups - 1 + jnp.where(t > 0, 1, 0) + jnp.where(t < tp - 1, 1, 0)
    )

    def own_send(c, to, send, recv):
        return pltpu.make_async_remote_copy(
            src_ref=acts.at[:, features(c)], dst_ref=gathered.at[t * chunks + c],
            send_sem=send.at[0, c], recv_sem=recv.at[0, c],
            device_id={"tp": to}, device_id_type=MESH,
        )

    def passed(j, s, c, to, send, recv):
        return pltpu.make_async_remote_copy(
            src_ref=gathered.at[j * chunks + c], dst_ref=gathered.at[j * chunks + c],
            send_sem=send.at[s, c], recv_sem=recv.at[s, c],
            device_id={"tp": to}, device_id_type=MESH,
        )

    @pl.loop(0, chunks)
    def _(c):
        @pl.when(t > 0)
        def _():
            own_send(c, t - 1, dn_send, dn_recv).start()

        @pl.when(t < tp - 1)
        def _():
            own_send(c, t + 1, up_send, up_recv).start()

    def factor_send(which, k):
        stage, work = (down_stage, down_work) if which == 0 else (up_stage, up_work)
        return pltpu.make_async_remote_copy(
            src_ref=stage.at[peer(k)], dst_ref=work.at[g],
            send_sem=fac_send.at[which, k - 1], recv_sem=fac_recv.at[which, k - 1],
            device_id={"grp": peer(k)}, device_id_type=MESH,
        )

    def factor_own(which):
        stage, work = (down_stage, down_work) if which == 0 else (up_stage, up_work)
        return pltpu.make_async_copy(stage.at[g], work.at[g], local_sem.at[2])

    @pl.loop(0, chunks)
    def _(c):
        own_copy(c).start()

    def pick(source, local, stage):
        piece = local.shape[2]

        @pl.loop(0, source.shape[2] // piece)
        def _(p):
            span = pl.ds(pl.multiple_of(p * piece, piece), piece)
            load = pltpu.make_async_copy(source.at[:, :, span], local, local_sem.at[1])
            load.start()
            load.wait()

            @pl.loop(0, groups)
            def _(d):
                for k in range(pair):
                    stage[d, k * rank:(k + 1) * rank, span] = local[pairings[g, k, d]]

    pick(down, down_local, down_stage)
    for k in range(1, groups):
        factor_send(0, k).start()
    factor_own(0).start()
    factor_own(0).wait()
    pick(up, up_local, up_stage)
    for k in range(1, groups):
        factor_send(1, k).start()
    factor_own(1).start()
    factor_own(1).wait()

    @pl.loop(0, tp)
    def _(j):
        weight_copy(j).start()

    @pl.loop(0, chunks)
    def _(c):
        own_copy(c).wait()

    @pl.loop(0, tp)
    def _(j):
        weight_copy(j).wait()

    tile = divisor(columns, 256)

    def product(j, c, first=False, last=False):
        @pl.loop(0, columns // tile)
        def _(n):
            span = pl.ds(pl.multiple_of(n * tile, tile), tile)
            value = jnp.dot(
                gathered[j * chunks + c], weights[j, features(c), span],
                preferred_element_type=jnp.float32,
            )
            if not first:
                value = acc[:, span] + value
            if last:
                staged[:, span] = value.astype(staged.dtype)
                out_copy(n).start()
            else:
                acc[:, span] = value

    def out_copy(n):
        span = pl.ds(pl.multiple_of(n * tile, tile), tile)
        return pltpu.make_async_copy(staged.at[:, span], out.at[:, span], out_sem.at[n])

    product(t, 0, True)

    @pl.loop(1, chunks)
    def _(c):
        product(t, c)

    for i in range(batch // 128):
        row = jnp.broadcast_to(slots[i:i + 1, :], (128, 128))
        slot_lanes[i * 128:(i + 1) * 128, :] = row.T

    for k in range(1, groups):
        factor_send(0, k).wait_recv()
    lane = lax.broadcasted_iota(jnp.int32, (batch, lanes), 1)
    lane_pair = lane // rank

    def one_group(s, total):
        def one_part(c, scores):
            return scores + lax.dot_general(
                gathered[t * chunks + c], down_work[s, :, features(c)], (((1,), (1,)), ((), ())),
                preferred_element_type=jnp.float32,
            )

        scores = lax.fori_loop(0, chunks, one_part, jnp.zeros((batch, lanes), jnp.float32))
        return total + jnp.where(slot_lanes[...] == s * pair + lane_pair, scores, 0.0)

    chosen = lax.fori_loop(0, groups, one_group, jnp.zeros((batch, lanes), jnp.float32))
    folded = chosen + pltpu.roll(chosen, rank, 1)
    low_lane = lax.broadcasted_iota(jnp.int32, (half, lanes), 1) < rank
    own_rank[...] = jnp.where(low_lane, folded[:half], folded[half:])

    def rank_pass(way, to):
        source, target = (low_out, low_in) if way == 0 else (high_out, high_in)
        return pltpu.make_async_remote_copy(
            src_ref=source, dst_ref=target,
            send_sem=rank_send.at[way], recv_sem=rank_recv.at[way],
            device_id={"tp": to}, device_id_type=MESH,
        )

    @pl.when(t == 0)
    def _():
        low_out[...] = own_rank[...]
        rank_pass(0, t + 1).start()

    @pl.when(t == tp - 1)
    def _():
        high_out[...] = own_rank[...]
        rank_pass(1, t - 1).start()

    def sum_pass(to):
        return pltpu.make_async_remote_copy(
            src_ref=sum_out, dst_ref=sum_in,
            send_sem=rank_send.at[2 + jnp.where(t > to, 1, 0)], recv_sem=rank_recv.at[2],
            device_id={"tp": to}, device_id_type=MESH,
        )

    inner = (t > 0) & (t < tp - 1)

    def rank_hop(s):
        @pl.when(inner & (t == s))
        def _():
            rank_pass(0, t).wait_recv()

            @pl.when(t < tp - 2)
            def _():
                low_out[...] = low_in[...] + own_rank[...]
                rank_pass(0, t + 1).start()

        @pl.when(inner & (t == tp - 1 - s))
        def _():
            rank_pass(1, t).wait_recv()

            @pl.when(t > 1)
            def _():
                high_out[...] = high_in[...] + own_rank[...]
                rank_pass(1, t - 1).start()

        @pl.when(inner & (s == tp - 2))
        def _():
            own_rank[...] += low_in[...] + high_in[...]
            sum_out[...] = own_rank[...].astype(sum_out.dtype)

            @pl.when(t == 1)
            def _():
                sum_pass(0).start()

            @pl.when(t == tp - 2)
            def _():
                sum_pass(tp - 1).start()

    def add_adapters():
        @pl.when(jnp.logical_not(inner))
        def _():
            sum_pass(t).wait_recv()
            own_rank[...] = sum_in[...].astype(jnp.float32)

        packed = own_rank[...]
        turned = pltpu.roll(packed, rank, 1)
        sums = jnp.concatenate(
            [jnp.where(low_lane, packed, turned), jnp.where(low_lane, turned, packed)], axis=0
        )
        for k in range(1, groups):
            factor_send(1, k).wait_recv()

        @pl.loop(0, groups)
        def _(s):
            spread = jnp.where(slot_lanes[...] == s * pair + lane_pair, sums, 0.0).astype(jnp.bfloat16)

            @pl.loop(0, columns // tile)
            def _(n):
                span = pl.ds(pl.multiple_of(n * tile, tile), tile)
                acc[:, span] += jnp.dot(
                    spread, up_work[s, :, span], preferred_element_type=jnp.float32
                )

    @pl.loop(1, tp)
    def _(s):
        @pl.loop(0, chunks)
        def _(c):
            @pl.when(t >= s)
            def _():
                passed(t - s, s - 1, c, t, up_send, up_recv).wait_recv()

                @pl.when(t < tp - 1)
                def _():
                    passed(t - s, s, c, t + 1, up_send, up_recv).start()

            @pl.when(t + s < tp)
            def _():
                passed(t + s, s - 1, c, t, dn_send, dn_recv).wait_recv()

                @pl.when(t > 0)
                def _():
                    passed(t + s, s, c, t - 1, dn_send, dn_recv).start()

            @pl.when(c == 0)
            def _():
                rank_hop(s)

                @pl.when(s == tp - 1)
                def _():
                    add_adapters()

            closing = (s == tp - 1) & (c == chunks - 1)

            @pl.when((t >= s) & jnp.logical_not(closing))
            def _():
                product(t - s, c)

            @pl.when((t + s < tp) & jnp.logical_not(closing))
            def _():
                product(t + s, c)

            @pl.when(closing & jnp.logical_not(inner))
            def _():
                product(tp - 1 - t, c, last=True)

            @pl.when(closing & inner)
            def _():
                @pl.loop(0, columns // tile)
                def _(n):
                    span = pl.ds(pl.multiple_of(n * tile, tile), tile)
                    staged[:, span] = acc[:, span].astype(staged.dtype)
                    out_copy(n).start()

    @pl.loop(0, tp)
    def _(s):
        @pl.loop(0, chunks)
        def _(c):
            @pl.when((t >= s) & (t < tp - 1))
            def _():
                passed(t, s, c, t, up_send, up_recv).wait_send()

            @pl.when((t + s < tp) & (t > 0))
            def _():
                passed(t, s, c, t, dn_send, dn_recv).wait_send()

    @pl.when(t < tp - 2)
    def _():
        rank_pass(0, t).wait_send()

    @pl.when(t > 1)
    def _():
        rank_pass(1, t).wait_send()

    @pl.when(t == 1)
    def _():
        sum_pass(0).wait_send()

    @pl.when(t == tp - 2)
    def _():
        sum_pass(tp - 1).wait_send()

    for which in range(2):
        for k in range(1, groups):
            factor_send(which, k).wait_send()

    @pl.loop(0, columns // tile)
    def _(n):
        out_copy(n).wait()


def body(tp, groups, acts, weight, down, up, pairings, slots):
    batch, depth = acts.shape
    columns = weight.shape[1]
    down = jnp.swapaxes(down, 1, 2)
    pairings = jnp.swapaxes(pairings, 1, 2)
    slots = slots.reshape(batch // 128, 128)
    held, rank, _ = down.shape
    lanes = pairings.shape[1] * rank
    part = divisor(depth, 256)
    chunks = depth // part
    tiles = columns // divisor(columns, 256)
    down_piece, up_piece = divisor(depth, 512), divisor(columns, 512)
    bf16, f32 = jnp.bfloat16, jnp.float32
    anywhere = pl.BlockSpec(memory_space=pl.ANY)
    flops = 2 * batch * columns * depth * tp + 2 * batch * groups * lanes * (depth + columns)
    packed = pltpu.VMEM((batch // 2, lanes), f32)
    return pl.pallas_call(
        functools.partial(kernel, tp, groups, chunks),
        out_shape=jax.ShapeDtypeStruct((batch, columns), bf16),
        in_specs=[anywhere] * 4
        + [pl.BlockSpec(memory_space=pltpu.SMEM), pl.BlockSpec(memory_space=pltpu.VMEM)],
        out_specs=anywhere,
        scratch_shapes=[
            pltpu.VMEM((tp * chunks, batch, part), bf16),
            pltpu.VMEM((tp, depth, columns), bf16),
            pltpu.VMEM((batch, columns), f32),
            pltpu.VMEM((held, rank, down_piece), bf16),
            pltpu.VMEM((held, rank, up_piece), bf16),
            pltpu.VMEM((groups, lanes, depth), bf16),
            pltpu.VMEM((groups, lanes, columns), bf16),
            pltpu.VMEM((groups, lanes, depth), bf16),
            pltpu.VMEM((groups, lanes, columns), bf16),
            packed, packed, packed, packed, packed,
            pltpu.VMEM((batch // 2, lanes), bf16),
            pltpu.VMEM((batch // 2, lanes), bf16),
            pltpu.VMEM((batch, lanes), jnp.int32),
            pltpu.VMEM((batch, columns), bf16),
            pltpu.SemaphoreType.DMA((tp, chunks)),
            pltpu.SemaphoreType.DMA((tp, chunks)),
            pltpu.SemaphoreType.DMA((tp, chunks)),
            pltpu.SemaphoreType.DMA((tp, chunks)),
            pltpu.SemaphoreType.DMA((2, groups)),
            pltpu.SemaphoreType.DMA((2, groups)),
            pltpu.SemaphoreType.DMA((4,)),
            pltpu.SemaphoreType.DMA((3,)),
            pltpu.SemaphoreType.DMA((tp,)),
            pltpu.SemaphoreType.DMA((chunks,)),
            pltpu.SemaphoreType.DMA((3,)),
            pltpu.SemaphoreType.DMA((tiles,)),
        ],
        compiler_params=pltpu.CompilerParams(
            collective_id=0, has_side_effects=True, vmem_limit_bytes=60 << 20
        ),
        cost_estimate=pl.CostEstimate(
            flops=flops, bytes_accessed=2 * (weight.size + 3 * acts.size), transcendentals=0
        ),
    )(acts, weight, down, up, pairings, slots)


def solution(mesh):
    placed = (
        P(("dom", "grp"), "tp"),
        P(None, "tp"),
        P("grp", "tp", None),
        P("grp", None, "tp"),
        P("dom", None, None),
        P(("dom", "grp")),
    )
    return jax.shard_map(
        functools.partial(body, mesh.shape["tp"], mesh.shape["grp"]),
        mesh=mesh, in_specs=placed, out_specs=P(("dom", "grp"), "tp"), check_vma=False,
    )
```

```python
import functools

import jax
import jax.numpy as jnp
from jax import lax
from jax.experimental import pallas as pl
from jax.experimental.pallas import tpu as pltpu
from jax.sharding import PartitionSpec as P

MESH = pl.DeviceIdType.MESH


def divisor(size, most):
    return most if size % most == 0 else size


def kernel(
    tp, groups, chunks,
    acts, weight, down, up, pairings, slots, out,
    gathered, weights, acc, down_local, up_local, down_stage, up_stage, down_work, up_work,
    own_rank, low_in, low_out, high_in, high_out, sum_in, sum_out, slot_lanes,
    up_send, up_recv, dn_send, dn_recv, fac_send, fac_recv, rank_send, rank_recv,
    weight_sem, own_sem, local_sem,
):
    g, t = lax.axis_index("grp"), lax.axis_index("tp")
    batch, depth = acts.shape
    columns = weight.shape[1]
    rank = down.shape[1]
    part = depth // chunks
    pair = pairings.shape[1]
    lanes = pair * rank
    half = batch // 2

    def features(c):
        return pl.ds(pl.multiple_of(c * part, part), part)

    def peer(k):
        return lax.rem(g + k, groups)

    def weight_copy(j):
        return pltpu.make_async_copy(
            weight.at[pl.ds(pl.multiple_of(j * depth, depth), depth), :], weights.at[j], weight_sem.at[j]
        )

    def own_copy(c):
        return pltpu.make_async_copy(acts.at[:, features(c)], gathered.at[t * chunks + c], own_sem.at[c])

    barrier = pltpu.get_barrier_semaphore()

    @pl.when(t > 0)
    def _():
        pl.semaphore_signal(barrier, inc=1, device_id={"tp": t - 1}, device_id_type=MESH)

    @pl.when(t < tp - 1)
    def _():
        pl.semaphore_signal(barrier, inc=1, device_id={"tp": t + 1}, device_id_type=MESH)

    for k in range(1, groups):
        pl.semaphore_signal(barrier, inc=1, device_id={"grp": peer(k)}, device_id_type=MESH)
    pl.semaphore_wait(
        barrier, groups - 1 + jnp.where(t > 0, 1, 0) + jnp.where(t < tp - 1, 1, 0)
    )

    def own_send(c, to, send, recv):
        return pltpu.make_async_remote_copy(
            src_ref=acts.at[:, features(c)], dst_ref=gathered.at[t * chunks + c],
            send_sem=send.at[0, c], recv_sem=recv.at[0, c],
            device_id={"tp": to}, device_id_type=MESH,
        )

    def passed(j, s, c, to, send, recv):
        return pltpu.make_async_remote_copy(
            src_ref=gathered.at[j * chunks + c], dst_ref=gathered.at[j * chunks + c],
            send_sem=send.at[s, c], recv_sem=recv.at[s, c],
            device_id={"tp": to}, device_id_type=MESH,
        )

    @pl.loop(0, chunks)
    def _(c):
        @pl.when(t > 0)
        def _():
            own_send(c, t - 1, dn_send, dn_recv).start()

        @pl.when(t < tp - 1)
        def _():
            own_send(c, t + 1, up_send, up_recv).start()

    def factor_send(which, k):
        stage, work = (down_stage, down_work) if which == 0 else (up_stage, up_work)
        return pltpu.make_async_remote_copy(
            src_ref=stage.at[peer(k)], dst_ref=work.at[g],
            send_sem=fac_send.at[which, k - 1], recv_sem=fac_recv.at[which, k - 1],
            device_id={"grp": peer(k)}, device_id_type=MESH,
        )

    def factor_own(which):
        stage, work = (down_stage, down_work) if which == 0 else (up_stage, up_work)
        return pltpu.make_async_copy(stage.at[g], work.at[g], local_sem.at[2])

    @pl.loop(0, chunks)
    def _(c):
        own_copy(c).start()

    def pick(source, local, stage):
        piece = local.shape[2]

        @pl.loop(0, source.shape[2] // piece)
        def _(p):
            span = pl.ds(pl.multiple_of(p * piece, piece), piece)
            load = pltpu.make_async_copy(source.at[:, :, span], local, local_sem.at[1])
            load.start()
            load.wait()

            @pl.loop(0, groups)
            def _(d):
                for k in range(pair):
                    stage[d, k * rank:(k + 1) * rank, span] = local[pairings[g, k, d]]

    pick(down, down_local, down_stage)
    for k in range(1, groups):
        factor_send(0, k).start()
    factor_own(0).start()
    factor_own(0).wait()
    pick(up, up_local, up_stage)
    for k in range(1, groups):
        factor_send(1, k).start()
    factor_own(1).start()
    factor_own(1).wait()

    @pl.loop(0, tp)
    def _(j):
        weight_copy(j).start()

    @pl.loop(0, chunks)
    def _(c):
        own_copy(c).wait()

    @pl.loop(0, tp)
    def _(j):
        weight_copy(j).wait()

    tile = divisor(columns, 256)

    def product(j, c, first=False, last=False):
        @pl.loop(0, columns // tile)
        def _(n):
            span = pl.ds(pl.multiple_of(n * tile, tile), tile)
            value = jnp.dot(
                gathered[j * chunks + c], weights[j, features(c), span],
                preferred_element_type=jnp.float32,
            )
            if not first:
                value = acc[:, span] + value
            if last:
                out[:, span] = value.astype(out.dtype)
            else:
                acc[:, span] = value

    product(t, 0, True)

    @pl.loop(1, chunks)
    def _(c):
        product(t, c)

    for i in range(batch // 128):
        row = jnp.broadcast_to(slots[i:i + 1, :], (128, 128))
        slot_lanes[i * 128:(i + 1) * 128, :] = row.T

    for k in range(1, groups):
        factor_send(0, k).wait_recv()
    lane = lax.broadcasted_iota(jnp.int32, (batch, lanes), 1)
    lane_pair = lane // rank

    def one_group(s, total):
        def one_part(c, scores):
            return scores + lax.dot_general(
                gathered[t * chunks + c], down_work[s, :, features(c)], (((1,), (1,)), ((), ())),
                preferred_element_type=jnp.float32,
            )

        scores = lax.fori_loop(0, chunks, one_part, jnp.zeros((batch, lanes), jnp.float32))
        return total + jnp.where(slot_lanes[...] == s * pair + lane_pair, scores, 0.0)

    chosen = lax.fori_loop(0, groups, one_group, jnp.zeros((batch, lanes), jnp.float32))
    folded = chosen + pltpu.roll(chosen, rank, 1)
    low_lane = lax.broadcasted_iota(jnp.int32, (half, lanes), 1) < rank
    own_rank[...] = jnp.where(low_lane, folded[:half], folded[half:])

    def rank_pass(way, to):
        source, target = (low_out, low_in) if way == 0 else (high_out, high_in)
        return pltpu.make_async_remote_copy(
            src_ref=source, dst_ref=target,
            send_sem=rank_send.at[way], recv_sem=rank_recv.at[way],
            device_id={"tp": to}, device_id_type=MESH,
        )

    @pl.when(t == 0)
    def _():
        low_out[...] = own_rank[...]
        rank_pass(0, t + 1).start()

    @pl.when(t == tp - 1)
    def _():
        high_out[...] = own_rank[...]
        rank_pass(1, t - 1).start()

    def sum_pass(to):
        return pltpu.make_async_remote_copy(
            src_ref=sum_out, dst_ref=sum_in,
            send_sem=rank_send.at[2 + jnp.where(t > to, 1, 0)], recv_sem=rank_recv.at[2],
            device_id={"tp": to}, device_id_type=MESH,
        )

    inner = (t > 0) & (t < tp - 1)

    def rank_hop(s):
        @pl.when(inner & (t == s))
        def _():
            rank_pass(0, t).wait_recv()

            @pl.when(t < tp - 2)
            def _():
                low_out[...] = low_in[...] + own_rank[...]
                rank_pass(0, t + 1).start()

        @pl.when(inner & (t == tp - 1 - s))
        def _():
            rank_pass(1, t).wait_recv()

            @pl.when(t > 1)
            def _():
                high_out[...] = high_in[...] + own_rank[...]
                rank_pass(1, t - 1).start()

        @pl.when(inner & (s == tp - 2))
        def _():
            own_rank[...] += low_in[...] + high_in[...]
            sum_out[...] = own_rank[...].astype(sum_out.dtype)

            @pl.when(t == 1)
            def _():
                sum_pass(0).start()

            @pl.when(t == tp - 2)
            def _():
                sum_pass(tp - 1).start()

    def add_adapters():
        @pl.when(jnp.logical_not(inner))
        def _():
            sum_pass(t).wait_recv()
            own_rank[...] = sum_in[...].astype(jnp.float32)

        packed = own_rank[...]
        turned = pltpu.roll(packed, rank, 1)
        sums = jnp.concatenate(
            [jnp.where(low_lane, packed, turned), jnp.where(low_lane, turned, packed)], axis=0
        )
        for k in range(1, groups):
            factor_send(1, k).wait_recv()

        @pl.loop(0, groups)
        def _(s):
            spread = jnp.where(slot_lanes[...] == s * pair + lane_pair, sums, 0.0).astype(jnp.bfloat16)

            @pl.loop(0, columns // tile)
            def _(n):
                span = pl.ds(pl.multiple_of(n * tile, tile), tile)
                acc[:, span] += jnp.dot(
                    spread, up_work[s, :, span], preferred_element_type=jnp.float32
                )

    @pl.loop(1, tp)
    def _(s):
        @pl.loop(0, chunks)
        def _(c):
            @pl.when(t >= s)
            def _():
                passed(t - s, s - 1, c, t, up_send, up_recv).wait_recv()

                @pl.when(t < tp - 1)
                def _():
                    passed(t - s, s, c, t + 1, up_send, up_recv).start()

            @pl.when(t + s < tp)
            def _():
                passed(t + s, s - 1, c, t, dn_send, dn_recv).wait_recv()

                @pl.when(t > 0)
                def _():
                    passed(t + s, s, c, t - 1, dn_send, dn_recv).start()

            @pl.when(c == 0)
            def _():
                rank_hop(s)

                @pl.when(s == tp - 1)
                def _():
                    add_adapters()

            closing = (s == tp - 1) & (c == chunks - 1)

            @pl.when((t >= s) & jnp.logical_not(closing))
            def _():
                product(t - s, c)

            @pl.when((t + s < tp) & jnp.logical_not(closing))
            def _():
                product(t + s, c)

            @pl.when(closing & jnp.logical_not(inner))
            def _():
                product(tp - 1 - t, c, last=True)

            @pl.when(closing & inner)
            def _():
                @pl.loop(0, columns // tile)
                def _(n):
                    span = pl.ds(pl.multiple_of(n * tile, tile), tile)
                    out[:, span] = acc[:, span].astype(out.dtype)

    @pl.loop(0, tp)
    def _(s):
        @pl.loop(0, chunks)
        def _(c):
            @pl.when((t >= s) & (t < tp - 1))
            def _():
                passed(t, s, c, t, up_send, up_recv).wait_send()

            @pl.when((t + s < tp) & (t > 0))
            def _():
                passed(t, s, c, t, dn_send, dn_recv).wait_send()

    @pl.when(t < tp - 2)
    def _():
        rank_pass(0, t).wait_send()

    @pl.when(t > 1)
    def _():
        rank_pass(1, t).wait_send()

    @pl.when(t == 1)
    def _():
        sum_pass(0).wait_send()

    @pl.when(t == tp - 2)
    def _():
        sum_pass(tp - 1).wait_send()

    for which in range(2):
        for k in range(1, groups):
            factor_send(which, k).wait_send()


def body(tp, groups, acts, weight, down, up, pairings, slots):
    batch, depth = acts.shape
    columns = weight.shape[1]
    down = jnp.swapaxes(down, 1, 2)
    pairings = jnp.swapaxes(pairings, 1, 2)
    slots = slots.reshape(batch // 128, 128)
    held, rank, _ = down.shape
    lanes = pairings.shape[1] * rank
    part = divisor(depth, 256)
    chunks = depth // part
    down_piece, up_piece = divisor(depth, 512), divisor(columns, 512)
    bf16, f32 = jnp.bfloat16, jnp.float32
    anywhere = pl.BlockSpec(memory_space=pl.ANY)
    flops = 2 * batch * columns * depth * tp + 2 * batch * groups * lanes * (depth + columns)
    packed = pltpu.VMEM((batch // 2, lanes), f32)
    return pl.pallas_call(
        functools.partial(kernel, tp, groups, chunks),
        out_shape=pltpu.VMEM((batch, columns), bf16),
        in_specs=[anywhere] * 4
        + [pl.BlockSpec(memory_space=pltpu.SMEM), pl.BlockSpec(memory_space=pltpu.VMEM)],
        out_specs=pl.BlockSpec(memory_space=pltpu.VMEM),
        scratch_shapes=[
            pltpu.VMEM((tp * chunks, batch, part), bf16),
            pltpu.VMEM((tp, depth, columns), bf16),
            pltpu.VMEM((batch, columns), f32),
            pltpu.VMEM((held, rank, down_piece), bf16),
            pltpu.VMEM((held, rank, up_piece), bf16),
            pltpu.VMEM((groups, lanes, depth), bf16),
            pltpu.VMEM((groups, lanes, columns), bf16),
            pltpu.VMEM((groups, lanes, depth), bf16),
            pltpu.VMEM((groups, lanes, columns), bf16),
            packed, packed, packed, packed, packed,
            pltpu.VMEM((batch // 2, lanes), bf16),
            pltpu.VMEM((batch // 2, lanes), bf16),
            pltpu.VMEM((batch, lanes), jnp.int32),
            pltpu.SemaphoreType.DMA((tp, chunks)),
            pltpu.SemaphoreType.DMA((tp, chunks)),
            pltpu.SemaphoreType.DMA((tp, chunks)),
            pltpu.SemaphoreType.DMA((tp, chunks)),
            pltpu.SemaphoreType.DMA((2, groups)),
            pltpu.SemaphoreType.DMA((2, groups)),
            pltpu.SemaphoreType.DMA((4,)),
            pltpu.SemaphoreType.DMA((3,)),
            pltpu.SemaphoreType.DMA((tp,)),
            pltpu.SemaphoreType.DMA((chunks,)),
            pltpu.SemaphoreType.DMA((3,)),
        ],
        compiler_params=pltpu.CompilerParams(
            collective_id=0, has_side_effects=True, vmem_limit_bytes=57 << 20
        ),
        cost_estimate=pl.CostEstimate(
            flops=flops, bytes_accessed=2 * (weight.size + 3 * acts.size), transcendentals=0
        ),
    )(acts, weight, down, up, pairings, slots)


def solution(mesh):
    placed = (
        P(("dom", "grp"), "tp"),
        P(None, "tp"),
        P("grp", "tp", None),
        P("grp", None, "tp"),
        P("dom", None, None),
        P(("dom", "grp")),
    )
    return jax.shard_map(
        functools.partial(body, mesh.shape["tp"], mesh.shape["grp"]),
        mesh=mesh, in_specs=placed, out_specs=P(("dom", "grp"), "tp"), check_vma=False,
    )
```

```python
import functools

import jax
import jax.numpy as jnp
from jax import lax
from jax.experimental import pallas as pl
from jax.experimental.pallas import tpu as pltpu
from jax.sharding import PartitionSpec as P

MESH = pl.DeviceIdType.MESH


def divisor(size, most):
    return most if size % most == 0 else size


def kernel(
    tp, groups, chunks,
    acts, weight, down, up, pairings, slots, out,
    gathered, weights, acc, down_local, up_local, down_stage, up_stage, down_work, up_work,
    own_rank, low_in, low_out, high_in, high_out, sum_in, sum_out, slot_lanes,
    up_send, up_recv, dn_send, dn_recv, fac_send, fac_recv, rank_send, rank_recv,
    weight_sem, own_sem, local_sem,
):
    g, t = lax.axis_index("grp"), lax.axis_index("tp")
    batch, depth = acts.shape
    columns = weight.shape[1]
    rank = down.shape[1]
    part = depth // chunks
    pair = pairings.shape[1]
    lanes = pair * rank
    half = batch // 2

    def features(c):
        return pl.ds(pl.multiple_of(c * part, part), part)

    def peer(k):
        return lax.rem(g + k, groups)

    def weight_copy(j):
        return pltpu.make_async_copy(
            weight.at[pl.ds(pl.multiple_of(j * depth, depth), depth), :], weights.at[j], weight_sem.at[j]
        )

    def own_copy(c):
        return pltpu.make_async_copy(acts.at[:, features(c)], gathered.at[t * chunks + c], own_sem.at[c])

    barrier = pltpu.get_barrier_semaphore()

    @pl.when(t > 0)
    def _():
        pl.semaphore_signal(barrier, inc=1, device_id={"tp": t - 1}, device_id_type=MESH)

    @pl.when(t < tp - 1)
    def _():
        pl.semaphore_signal(barrier, inc=1, device_id={"tp": t + 1}, device_id_type=MESH)

    for k in range(1, groups):
        pl.semaphore_signal(barrier, inc=1, device_id={"grp": peer(k)}, device_id_type=MESH)
    pl.semaphore_wait(
        barrier, groups - 1 + jnp.where(t > 0, 1, 0) + jnp.where(t < tp - 1, 1, 0)
    )

    def own_send(c, to, send, recv):
        return pltpu.make_async_remote_copy(
            src_ref=acts.at[:, features(c)], dst_ref=gathered.at[t * chunks + c],
            send_sem=send.at[0, c], recv_sem=recv.at[0, c],
            device_id={"tp": to}, device_id_type=MESH,
        )

    def passed(j, s, c, to, send, recv):
        return pltpu.make_async_remote_copy(
            src_ref=gathered.at[j * chunks + c], dst_ref=gathered.at[j * chunks + c],
            send_sem=send.at[s, c], recv_sem=recv.at[s, c],
            device_id={"tp": to}, device_id_type=MESH,
        )

    @pl.loop(0, chunks)
    def _(c):
        @pl.when(t > 0)
        def _():
            own_send(c, t - 1, dn_send, dn_recv).start()

        @pl.when(t < tp - 1)
        def _():
            own_send(c, t + 1, up_send, up_recv).start()

    def factor_send(which, k):
        stage, work = (down_stage, down_work) if which == 0 else (up_stage, up_work)
        return pltpu.make_async_remote_copy(
            src_ref=stage.at[peer(k)], dst_ref=work.at[g],
            send_sem=fac_send.at[which, k - 1], recv_sem=fac_recv.at[which, k - 1],
            device_id={"grp": peer(k)}, device_id_type=MESH,
        )

    def factor_own(which):
        stage, work = (down_stage, down_work) if which == 0 else (up_stage, up_work)
        return pltpu.make_async_copy(stage.at[g], work.at[g], local_sem.at[2])

    @pl.loop(0, chunks)
    def _(c):
        own_copy(c).start()

    def pick(source, local, stage):
        piece = local.shape[2]

        @pl.loop(0, source.shape[2] // piece)
        def _(p):
            span = pl.ds(pl.multiple_of(p * piece, piece), piece)
            load = pltpu.make_async_copy(source.at[:, :, span], local, local_sem.at[1])
            load.start()
            load.wait()

            @pl.loop(0, groups)
            def _(d):
                for k in range(pair):
                    stage[d, k * rank:(k + 1) * rank, span] = local[pairings[g, k, d]]

    pick(down, down_local, down_stage)
    for k in range(1, groups):
        factor_send(0, k).start()
    factor_own(0).start()
    factor_own(0).wait()
    pick(up, up_local, up_stage)
    for k in range(1, groups):
        factor_send(1, k).start()
    factor_own(1).start()
    factor_own(1).wait()

    @pl.loop(0, tp)
    def _(j):
        weight_copy(j).start()

    @pl.loop(0, chunks)
    def _(c):
        own_copy(c).wait()

    @pl.loop(0, tp)
    def _(j):
        weight_copy(j).wait()

    tile = divisor(columns, 256)

    def product(j, c, first=False, last=False):
        @pl.loop(0, columns // tile)
        def _(n):
            span = pl.ds(pl.multiple_of(n * tile, tile), tile)
            value = jnp.dot(
                gathered[j * chunks + c], weights[j, features(c), span],
                preferred_element_type=jnp.float32,
            )
            if not first:
                value = acc[:, span] + value
            if last:
                out[:, span] = value.astype(out.dtype)
            else:
                acc[:, span] = value

    product(t, 0, True)

    @pl.loop(1, chunks)
    def _(c):
        product(t, c)

    for i in range(batch // 128):
        row = jnp.broadcast_to(slots[i:i + 1, :], (128, 128))
        slot_lanes[i * 128:(i + 1) * 128, :] = row.T

    for k in range(1, groups):
        factor_send(0, k).wait_recv()
    lane = lax.broadcasted_iota(jnp.int32, (batch, lanes), 1)
    lane_pair = lane // rank

    def one_group(s, total):
        def one_part(c, scores):
            return scores + lax.dot_general(
                gathered[t * chunks + c], down_work[s, :, features(c)], (((1,), (1,)), ((), ())),
                preferred_element_type=jnp.float32,
            )

        scores = lax.fori_loop(0, chunks, one_part, jnp.zeros((batch, lanes), jnp.float32))
        return total + jnp.where(slot_lanes[...] == s * pair + lane_pair, scores, 0.0)

    chosen = lax.fori_loop(0, groups, one_group, jnp.zeros((batch, lanes), jnp.float32))
    folded = chosen + pltpu.roll(chosen, rank, 1)
    low_lane = lax.broadcasted_iota(jnp.int32, (half, lanes), 1) < rank
    own_rank[...] = jnp.where(low_lane, folded[:half], folded[half:])

    def rank_pass(way, to):
        source, target = (low_out, low_in) if way == 0 else (high_out, high_in)
        return pltpu.make_async_remote_copy(
            src_ref=source, dst_ref=target,
            send_sem=rank_send.at[way], recv_sem=rank_recv.at[way],
            device_id={"tp": to}, device_id_type=MESH,
        )

    @pl.when(t == 0)
    def _():
        low_out[...] = own_rank[...]
        rank_pass(0, t + 1).start()

    @pl.when(t == tp - 1)
    def _():
        high_out[...] = own_rank[...]
        rank_pass(1, t - 1).start()

    def sum_pass(to):
        return pltpu.make_async_remote_copy(
            src_ref=sum_out, dst_ref=sum_in,
            send_sem=rank_send.at[2 + jnp.where(t > to, 1, 0)], recv_sem=rank_recv.at[2],
            device_id={"tp": to}, device_id_type=MESH,
        )

    inner = (t > 0) & (t < tp - 1)

    def rank_hop(s):
        @pl.when(inner & (t == s))
        def _():
            rank_pass(0, t).wait_recv()

            @pl.when(t < tp - 2)
            def _():
                low_out[...] = low_in[...] + own_rank[...]
                rank_pass(0, t + 1).start()

        @pl.when(inner & (t == tp - 1 - s))
        def _():
            rank_pass(1, t).wait_recv()

            @pl.when(t > 1)
            def _():
                high_out[...] = high_in[...] + own_rank[...]
                rank_pass(1, t - 1).start()

        @pl.when(inner & (s == tp - 2))
        def _():
            own_rank[...] += low_in[...] + high_in[...]
            sum_out[...] = own_rank[...].astype(sum_out.dtype)

            @pl.when(t == 1)
            def _():
                sum_pass(0).start()

            @pl.when(t == tp - 2)
            def _():
                sum_pass(tp - 1).start()

    def add_adapters():
        @pl.when(jnp.logical_not(inner))
        def _():
            sum_pass(t).wait_recv()
            own_rank[...] = sum_in[...].astype(jnp.float32)

        packed = own_rank[...]
        turned = pltpu.roll(packed, rank, 1)
        sums = jnp.concatenate(
            [jnp.where(low_lane, packed, turned), jnp.where(low_lane, turned, packed)], axis=0
        )
        for k in range(1, groups):
            factor_send(1, k).wait_recv()

        @pl.loop(0, groups)
        def _(s):
            spread = jnp.where(slot_lanes[...] == s * pair + lane_pair, sums, 0.0).astype(jnp.bfloat16)

            @pl.loop(0, columns // tile)
            def _(n):
                span = pl.ds(pl.multiple_of(n * tile, tile), tile)
                acc[:, span] += jnp.dot(
                    spread, up_work[s, :, span], preferred_element_type=jnp.float32
                )

    flight = min(2, chunks)

    @pl.loop(1, tp)
    def _(s):
        @pl.loop(0, chunks)
        def _(c):
            paced = (s == tp - 2) & (c >= flight)

            @pl.when(t >= s)
            def _():
                passed(t - s, s - 1, c, t, up_send, up_recv).wait_recv()

                @pl.when((t < tp - 1) & paced)
                def _():
                    passed(t, s, c - flight, t, up_send, up_recv).wait_send()

                @pl.when(t < tp - 1)
                def _():
                    passed(t - s, s, c, t + 1, up_send, up_recv).start()

            @pl.when(t + s < tp)
            def _():
                passed(t + s, s - 1, c, t, dn_send, dn_recv).wait_recv()

                @pl.when((t > 0) & paced)
                def _():
                    passed(t, s, c - flight, t, dn_send, dn_recv).wait_send()

                @pl.when(t > 0)
                def _():
                    passed(t + s, s, c, t - 1, dn_send, dn_recv).start()

            @pl.when(c == 0)
            def _():
                rank_hop(s)

                @pl.when(s == tp - 1)
                def _():
                    add_adapters()

            closing = (s == tp - 1) & (c == chunks - 1)

            @pl.when((t >= s) & jnp.logical_not(closing))
            def _():
                product(t - s, c)

            @pl.when((t + s < tp) & jnp.logical_not(closing))
            def _():
                product(t + s, c)

            @pl.when(closing & jnp.logical_not(inner))
            def _():
                product(tp - 1 - t, c, last=True)

            @pl.when(closing & inner)
            def _():
                @pl.loop(0, columns // tile)
                def _(n):
                    span = pl.ds(pl.multiple_of(n * tile, tile), tile)
                    out[:, span] = acc[:, span].astype(out.dtype)

    @pl.loop(0, tp)
    def _(s):
        @pl.loop(0, chunks)
        def _(c):
            left = (s != tp - 2) | (c >= chunks - flight)

            @pl.when((t >= s) & (t < tp - 1) & left)
            def _():
                passed(t, s, c, t, up_send, up_recv).wait_send()

            @pl.when((t + s < tp) & (t > 0) & left)
            def _():
                passed(t, s, c, t, dn_send, dn_recv).wait_send()

    @pl.when(t < tp - 2)
    def _():
        rank_pass(0, t).wait_send()

    @pl.when(t > 1)
    def _():
        rank_pass(1, t).wait_send()

    @pl.when(t == 1)
    def _():
        sum_pass(0).wait_send()

    @pl.when(t == tp - 2)
    def _():
        sum_pass(tp - 1).wait_send()

    for which in range(2):
        for k in range(1, groups):
            factor_send(which, k).wait_send()


def body(tp, groups, acts, weight, down, up, pairings, slots):
    batch, depth = acts.shape
    columns = weight.shape[1]
    down = jnp.swapaxes(down, 1, 2)
    pairings = jnp.swapaxes(pairings, 1, 2)
    slots = slots.reshape(batch // 128, 128)
    held, rank, _ = down.shape
    lanes = pairings.shape[1] * rank
    part = divisor(depth, 256)
    chunks = depth // part
    down_piece, up_piece = divisor(depth, 512), divisor(columns, 512)
    bf16, f32 = jnp.bfloat16, jnp.float32
    anywhere = pl.BlockSpec(memory_space=pl.ANY)
    flops = 2 * batch * columns * depth * tp + 2 * batch * groups * lanes * (depth + columns)
    packed = pltpu.VMEM((batch // 2, lanes), f32)
    return pl.pallas_call(
        functools.partial(kernel, tp, groups, chunks),
        out_shape=pltpu.VMEM((batch, columns), bf16),
        in_specs=[anywhere] * 4
        + [pl.BlockSpec(memory_space=pltpu.SMEM), pl.BlockSpec(memory_space=pltpu.VMEM)],
        out_specs=pl.BlockSpec(memory_space=pltpu.VMEM),
        scratch_shapes=[
            pltpu.VMEM((tp * chunks, batch, part), bf16),
            pltpu.VMEM((tp, depth, columns), bf16),
            pltpu.VMEM((batch, columns), f32),
            pltpu.VMEM((held, rank, down_piece), bf16),
            pltpu.VMEM((held, rank, up_piece), bf16),
            pltpu.VMEM((groups, lanes, depth), bf16),
            pltpu.VMEM((groups, lanes, columns), bf16),
            pltpu.VMEM((groups, lanes, depth), bf16),
            pltpu.VMEM((groups, lanes, columns), bf16),
            packed, packed, packed, packed, packed,
            pltpu.VMEM((batch // 2, lanes), bf16),
            pltpu.VMEM((batch // 2, lanes), bf16),
            pltpu.VMEM((batch, lanes), jnp.int32),
            pltpu.SemaphoreType.DMA((tp, chunks)),
            pltpu.SemaphoreType.DMA((tp, chunks)),
            pltpu.SemaphoreType.DMA((tp, chunks)),
            pltpu.SemaphoreType.DMA((tp, chunks)),
            pltpu.SemaphoreType.DMA((2, groups)),
            pltpu.SemaphoreType.DMA((2, groups)),
            pltpu.SemaphoreType.DMA((4,)),
            pltpu.SemaphoreType.DMA((3,)),
            pltpu.SemaphoreType.DMA((tp,)),
            pltpu.SemaphoreType.DMA((chunks,)),
            pltpu.SemaphoreType.DMA((3,)),
        ],
        compiler_params=pltpu.CompilerParams(
            collective_id=0, has_side_effects=True, vmem_limit_bytes=57 << 20
        ),
        cost_estimate=pl.CostEstimate(
            flops=flops, bytes_accessed=2 * (weight.size + 3 * acts.size), transcendentals=0
        ),
    )(acts, weight, down, up, pairings, slots)


def solution(mesh):
    placed = (
        P(("dom", "grp"), "tp"),
        P(None, "tp"),
        P("grp", "tp", None),
        P("grp", None, "tp"),
        P("dom", None, None),
        P(("dom", "grp")),
    )
    return jax.shard_map(
        functools.partial(body, mesh.shape["tp"], mesh.shape["grp"]),
        mesh=mesh, in_specs=placed, out_specs=P(("dom", "grp"), "tp"), check_vma=False,
    )
```

```python
import functools

import jax
import jax.numpy as jnp
from jax import lax
from jax.experimental import pallas as pl
from jax.experimental.pallas import tpu as pltpu
from jax.sharding import PartitionSpec as P

MESH = pl.DeviceIdType.MESH


def divisor(size, most):
    return most if size % most == 0 else size


def kernel(
    tp, groups, chunks,
    acts, weight, down, up, pairings, slots, out,
    gathered, weights, acc, down_local, up_local, down_stage, up_stage, down_work, up_work,
    own_rank, low_in, low_out, high_in, high_out, sum_in, sum_out, slot_lanes,
    up_send, up_recv, dn_send, dn_recv, fac_send, fac_recv, rank_send, rank_recv,
    weight_sem, own_sem, local_sem,
):
    g, t = lax.axis_index("grp"), lax.axis_index("tp")
    batch, depth = acts.shape
    columns = weight.shape[1]
    rank = down.shape[1]
    part = depth // chunks
    pair = pairings.shape[1]
    lanes = pair * rank
    half = batch // 2

    def features(c):
        return pl.ds(pl.multiple_of(c * part, part), part)

    def peer(k):
        return lax.rem(g + k, groups)

    def weight_copy(j):
        return pltpu.make_async_copy(
            weight.at[pl.ds(pl.multiple_of(j * depth, depth), depth), :], weights.at[j], weight_sem.at[j]
        )

    def own_copy(c):
        return pltpu.make_async_copy(acts.at[:, features(c)], gathered.at[t * chunks + c], own_sem.at[c])

    barrier = pltpu.get_barrier_semaphore()

    @pl.when(t > 0)
    def _():
        pl.semaphore_signal(barrier, inc=1, device_id={"tp": t - 1}, device_id_type=MESH)

    @pl.when(t < tp - 1)
    def _():
        pl.semaphore_signal(barrier, inc=1, device_id={"tp": t + 1}, device_id_type=MESH)

    for k in range(1, groups):
        pl.semaphore_signal(barrier, inc=1, device_id={"grp": peer(k)}, device_id_type=MESH)
    pl.semaphore_wait(
        barrier, groups - 1 + jnp.where(t > 0, 1, 0) + jnp.where(t < tp - 1, 1, 0)
    )

    def own_send(c, to, send, recv):
        return pltpu.make_async_remote_copy(
            src_ref=acts.at[:, features(c)], dst_ref=gathered.at[t * chunks + c],
            send_sem=send.at[0, c], recv_sem=recv.at[0, c],
            device_id={"tp": to}, device_id_type=MESH,
        )

    def passed(j, s, c, to, send, recv):
        return pltpu.make_async_remote_copy(
            src_ref=gathered.at[j * chunks + c], dst_ref=gathered.at[j * chunks + c],
            send_sem=send.at[s, c], recv_sem=recv.at[s, c],
            device_id={"tp": to}, device_id_type=MESH,
        )

    @pl.loop(0, chunks)
    def _(c):
        @pl.when(t > 0)
        def _():
            own_send(c, t - 1, dn_send, dn_recv).start()

        @pl.when(t < tp - 1)
        def _():
            own_send(c, t + 1, up_send, up_recv).start()

    def factor_send(which, k):
        stage, work = (down_stage, down_work) if which == 0 else (up_stage, up_work)
        return pltpu.make_async_remote_copy(
            src_ref=stage.at[peer(k)], dst_ref=work.at[g],
            send_sem=fac_send.at[which, k - 1], recv_sem=fac_recv.at[which, k - 1],
            device_id={"grp": peer(k)}, device_id_type=MESH,
        )

    def factor_own(which):
        stage, work = (down_stage, down_work) if which == 0 else (up_stage, up_work)
        return pltpu.make_async_copy(stage.at[g], work.at[g], local_sem.at[2])

    @pl.loop(0, chunks)
    def _(c):
        own_copy(c).start()

    def pick(source, local, stage):
        piece = local.shape[2]

        @pl.loop(0, source.shape[2] // piece)
        def _(p):
            span = pl.ds(pl.multiple_of(p * piece, piece), piece)
            load = pltpu.make_async_copy(source.at[:, :, span], local, local_sem.at[1])
            load.start()
            load.wait()

            @pl.loop(0, groups)
            def _(d):
                for k in range(pair):
                    stage[d, k * rank:(k + 1) * rank, span] = local[pairings[g, k, d]]

    pick(down, down_local, down_stage)
    for k in range(1, groups):
        factor_send(0, k).start()
    factor_own(0).start()
    factor_own(0).wait()
    pick(up, up_local, up_stage)
    for k in range(1, groups):
        factor_send(1, k).start()
    factor_own(1).start()
    factor_own(1).wait()

    @pl.loop(0, tp)
    def _(j):
        weight_copy(j).start()

    @pl.loop(0, chunks)
    def _(c):
        own_copy(c).wait()

    @pl.loop(0, tp)
    def _(j):
        weight_copy(j).wait()

    tile = divisor(columns, 512)

    def product(j, c, first=False, last=False):
        @pl.loop(0, columns // tile)
        def _(n):
            span = pl.ds(pl.multiple_of(n * tile, tile), tile)
            value = jnp.dot(
                gathered[j * chunks + c], weights[j, features(c), span],
                preferred_element_type=jnp.float32,
            )
            if not first:
                value = acc[:, span] + value
            if last:
                out[:, span] = value.astype(out.dtype)
            else:
                acc[:, span] = value

    product(t, 0, True)

    @pl.loop(1, chunks)
    def _(c):
        product(t, c)

    for i in range(batch // 128):
        row = jnp.broadcast_to(slots[i:i + 1, :], (128, 128))
        slot_lanes[i * 128:(i + 1) * 128, :] = row.T

    for k in range(1, groups):
        factor_send(0, k).wait_recv()
    lane = lax.broadcasted_iota(jnp.int32, (batch, lanes), 1)
    lane_pair = lane // rank

    def one_group(s, total):
        def one_part(c, scores):
            return scores + lax.dot_general(
                gathered[t * chunks + c], down_work[s, :, features(c)], (((1,), (1,)), ((), ())),
                preferred_element_type=jnp.float32,
            )

        scores = lax.fori_loop(0, chunks, one_part, jnp.zeros((batch, lanes), jnp.float32))
        return total + jnp.where(slot_lanes[...] == s * pair + lane_pair, scores, 0.0)

    chosen = lax.fori_loop(0, groups, one_group, jnp.zeros((batch, lanes), jnp.float32))
    folded = chosen + pltpu.roll(chosen, rank, 1)
    low_lane = lax.broadcasted_iota(jnp.int32, (half, lanes), 1) < rank
    own_rank[...] = jnp.where(low_lane, folded[:half], folded[half:])

    def rank_pass(way, to):
        source, target = (low_out, low_in) if way == 0 else (high_out, high_in)
        return pltpu.make_async_remote_copy(
            src_ref=source, dst_ref=target,
            send_sem=rank_send.at[way], recv_sem=rank_recv.at[way],
            device_id={"tp": to}, device_id_type=MESH,
        )

    @pl.when(t == 0)
    def _():
        low_out[...] = own_rank[...]
        rank_pass(0, t + 1).start()

    @pl.when(t == tp - 1)
    def _():
        high_out[...] = own_rank[...]
        rank_pass(1, t - 1).start()

    def sum_pass(to):
        return pltpu.make_async_remote_copy(
            src_ref=sum_out, dst_ref=sum_in,
            send_sem=rank_send.at[2 + jnp.where(t > to, 1, 0)], recv_sem=rank_recv.at[2],
            device_id={"tp": to}, device_id_type=MESH,
        )

    inner = (t > 0) & (t < tp - 1)

    def rank_hop(s):
        @pl.when(inner & (t == s))
        def _():
            rank_pass(0, t).wait_recv()

            @pl.when(t < tp - 2)
            def _():
                low_out[...] = low_in[...] + own_rank[...]
                rank_pass(0, t + 1).start()

        @pl.when(inner & (t == tp - 1 - s))
        def _():
            rank_pass(1, t).wait_recv()

            @pl.when(t > 1)
            def _():
                high_out[...] = high_in[...] + own_rank[...]
                rank_pass(1, t - 1).start()

        @pl.when(inner & (s == tp - 2))
        def _():
            own_rank[...] += low_in[...] + high_in[...]
            sum_out[...] = own_rank[...].astype(sum_out.dtype)

            @pl.when(t == 1)
            def _():
                sum_pass(0).start()

            @pl.when(t == tp - 2)
            def _():
                sum_pass(tp - 1).start()

    def add_adapters():
        @pl.when(jnp.logical_not(inner))
        def _():
            sum_pass(t).wait_recv()
            own_rank[...] = sum_in[...].astype(jnp.float32)

        packed = own_rank[...]
        turned = pltpu.roll(packed, rank, 1)
        sums = jnp.concatenate(
            [jnp.where(low_lane, packed, turned), jnp.where(low_lane, turned, packed)], axis=0
        )
        for k in range(1, groups):
            factor_send(1, k).wait_recv()

        @pl.loop(0, groups)
        def _(s):
            spread = jnp.where(slot_lanes[...] == s * pair + lane_pair, sums, 0.0).astype(jnp.bfloat16)

            @pl.loop(0, columns // tile)
            def _(n):
                span = pl.ds(pl.multiple_of(n * tile, tile), tile)
                acc[:, span] += jnp.dot(
                    spread, up_work[s, :, span], preferred_element_type=jnp.float32
                )

    @pl.loop(1, tp)
    def _(s):
        @pl.loop(0, chunks)
        def _(c):
            @pl.when(t >= s)
            def _():
                passed(t - s, s - 1, c, t, up_send, up_recv).wait_recv()

                @pl.when(t < tp - 1)
                def _():
                    passed(t - s, s, c, t + 1, up_send, up_recv).start()

            @pl.when(t + s < tp)
            def _():
                passed(t + s, s - 1, c, t, dn_send, dn_recv).wait_recv()

                @pl.when(t > 0)
                def _():
                    passed(t + s, s, c, t - 1, dn_send, dn_recv).start()

            @pl.when(c == 0)
            def _():
                rank_hop(s)

                @pl.when(s == tp - 1)
                def _():
                    add_adapters()

            closing = (s == tp - 1) & (c == chunks - 1)

            @pl.when((t >= s) & jnp.logical_not(closing))
            def _():
                product(t - s, c)

            @pl.when((t + s < tp) & jnp.logical_not(closing))
            def _():
                product(t + s, c)

            @pl.when(closing & jnp.logical_not(inner))
            def _():
                product(tp - 1 - t, c, last=True)

            @pl.when(closing & inner)
            def _():
                @pl.loop(0, columns // tile)
                def _(n):
                    span = pl.ds(pl.multiple_of(n * tile, tile), tile)
                    out[:, span] = acc[:, span].astype(out.dtype)

    @pl.loop(0, tp)
    def _(s):
        @pl.loop(0, chunks)
        def _(c):
            @pl.when((t >= s) & (t < tp - 1))
            def _():
                passed(t, s, c, t, up_send, up_recv).wait_send()

            @pl.when((t + s < tp) & (t > 0))
            def _():
                passed(t, s, c, t, dn_send, dn_recv).wait_send()

    @pl.when(t < tp - 2)
    def _():
        rank_pass(0, t).wait_send()

    @pl.when(t > 1)
    def _():
        rank_pass(1, t).wait_send()

    @pl.when(t == 1)
    def _():
        sum_pass(0).wait_send()

    @pl.when(t == tp - 2)
    def _():
        sum_pass(tp - 1).wait_send()

    for which in range(2):
        for k in range(1, groups):
            factor_send(which, k).wait_send()


def body(tp, groups, acts, weight, down, up, pairings, slots):
    batch, depth = acts.shape
    columns = weight.shape[1]
    down = jnp.swapaxes(down, 1, 2)
    pairings = jnp.swapaxes(pairings, 1, 2)
    slots = slots.reshape(batch // 128, 128)
    held, rank, _ = down.shape
    lanes = pairings.shape[1] * rank
    part = divisor(depth, 256)
    chunks = depth // part
    down_piece, up_piece = divisor(depth, 512), divisor(columns, 512)
    bf16, f32 = jnp.bfloat16, jnp.float32
    anywhere = pl.BlockSpec(memory_space=pl.ANY)
    flops = 2 * batch * columns * depth * tp + 2 * batch * groups * lanes * (depth + columns)
    packed = pltpu.VMEM((batch // 2, lanes), f32)
    return pl.pallas_call(
        functools.partial(kernel, tp, groups, chunks),
        out_shape=pltpu.VMEM((batch, columns), bf16),
        in_specs=[anywhere] * 4
        + [pl.BlockSpec(memory_space=pltpu.SMEM), pl.BlockSpec(memory_space=pltpu.VMEM)],
        out_specs=pl.BlockSpec(memory_space=pltpu.VMEM),
        scratch_shapes=[
            pltpu.VMEM((tp * chunks, batch, part), bf16),
            pltpu.VMEM((tp, depth, columns), bf16),
            pltpu.VMEM((batch, columns), f32),
            pltpu.VMEM((held, rank, down_piece), bf16),
            pltpu.VMEM((held, rank, up_piece), bf16),
            pltpu.VMEM((groups, lanes, depth), bf16),
            pltpu.VMEM((groups, lanes, columns), bf16),
            pltpu.VMEM((groups, lanes, depth), bf16),
            pltpu.VMEM((groups, lanes, columns), bf16),
            packed, packed, packed, packed, packed,
            pltpu.VMEM((batch // 2, lanes), bf16),
            pltpu.VMEM((batch // 2, lanes), bf16),
            pltpu.VMEM((batch, lanes), jnp.int32),
            pltpu.SemaphoreType.DMA((tp, chunks)),
            pltpu.SemaphoreType.DMA((tp, chunks)),
            pltpu.SemaphoreType.DMA((tp, chunks)),
            pltpu.SemaphoreType.DMA((tp, chunks)),
            pltpu.SemaphoreType.DMA((2, groups)),
            pltpu.SemaphoreType.DMA((2, groups)),
            pltpu.SemaphoreType.DMA((4,)),
            pltpu.SemaphoreType.DMA((3,)),
            pltpu.SemaphoreType.DMA((tp,)),
            pltpu.SemaphoreType.DMA((chunks,)),
            pltpu.SemaphoreType.DMA((3,)),
        ],
        compiler_params=pltpu.CompilerParams(
            collective_id=0, has_side_effects=True, vmem_limit_bytes=57 << 20
        ),
        cost_estimate=pl.CostEstimate(
            flops=flops, bytes_accessed=2 * (weight.size + 3 * acts.size), transcendentals=0
        ),
    )(acts, weight, down, up, pairings, slots)


def solution(mesh):
    placed = (
        P(("dom", "grp"), "tp"),
        P(None, "tp"),
        P("grp", "tp", None),
        P("grp", None, "tp"),
        P("dom", None, None),
        P(("dom", "grp")),
    )
    return jax.shard_map(
        functools.partial(body, mesh.shape["tp"], mesh.shape["grp"]),
        mesh=mesh, in_specs=placed, out_specs=P(("dom", "grp"), "tp"), check_vma=False,
    )
```

```python
import functools

import jax
import jax.numpy as jnp
from jax import lax
from jax.experimental import pallas as pl
from jax.experimental.pallas import tpu as pltpu
from jax.sharding import PartitionSpec as P

MESH = pl.DeviceIdType.MESH


def divisor(size, most):
    return most if size % most == 0 else size


def kernel(
    tp, groups, chunks,
    acts, weight, down, up, pairings, slots, out,
    gathered, weights, acc, down_local, up_local, down_stage, up_stage, down_work, up_work,
    own_rank, low_in, low_out, high_in, high_out, sum_in, sum_out, slot_lanes,
    up_send, up_recv, dn_send, dn_recv, fac_send, fac_recv, rank_send, rank_recv,
    weight_sem, own_sem, local_sem,
):
    g, t = lax.axis_index("grp"), lax.axis_index("tp")
    batch, depth = acts.shape
    columns = weight.shape[1]
    rank = down.shape[1]
    part = depth // chunks
    pair = pairings.shape[1]
    lanes = pair * rank
    half = batch // 2

    def features(c):
        return pl.ds(pl.multiple_of(c * part, part), part)

    def peer(k):
        return lax.rem(g + k, groups)

    def weight_copy(j):
        return pltpu.make_async_copy(
            weight.at[pl.ds(pl.multiple_of(j * depth, depth), depth), :], weights.at[j], weight_sem.at[j]
        )

    def own_copy(c):
        return pltpu.make_async_copy(acts.at[:, features(c)], gathered.at[t * chunks + c], own_sem.at[c])

    barrier = pltpu.get_barrier_semaphore()

    @pl.when(t > 0)
    def _():
        pl.semaphore_signal(barrier, inc=1, device_id={"tp": t - 1}, device_id_type=MESH)

    @pl.when(t < tp - 1)
    def _():
        pl.semaphore_signal(barrier, inc=1, device_id={"tp": t + 1}, device_id_type=MESH)

    for k in range(1, groups):
        pl.semaphore_signal(barrier, inc=1, device_id={"grp": peer(k)}, device_id_type=MESH)
    pl.semaphore_wait(
        barrier, groups - 1 + jnp.where(t > 0, 1, 0) + jnp.where(t < tp - 1, 1, 0)
    )

    def own_send(c, to, send, recv):
        return pltpu.make_async_remote_copy(
            src_ref=acts.at[:, features(c)], dst_ref=gathered.at[t * chunks + c],
            send_sem=send.at[0, c], recv_sem=recv.at[0, c],
            device_id={"tp": to}, device_id_type=MESH,
        )

    def passed(j, s, c, to, send, recv):
        return pltpu.make_async_remote_copy(
            src_ref=gathered.at[j * chunks + c], dst_ref=gathered.at[j * chunks + c],
            send_sem=send.at[s, c], recv_sem=recv.at[s, c],
            device_id={"tp": to}, device_id_type=MESH,
        )

    @pl.loop(0, chunks)
    def _(c):
        @pl.when(t > 0)
        def _():
            own_send(c, t - 1, dn_send, dn_recv).start()

        @pl.when(t < tp - 1)
        def _():
            own_send(c, t + 1, up_send, up_recv).start()

    def factor_send(which, k):
        stage, work = (down_stage, down_work) if which == 0 else (up_stage, up_work)
        return pltpu.make_async_remote_copy(
            src_ref=stage.at[peer(k)], dst_ref=work.at[g],
            send_sem=fac_send.at[which, k - 1], recv_sem=fac_recv.at[which, k - 1],
            device_id={"grp": peer(k)}, device_id_type=MESH,
        )

    def factor_own(which):
        stage, work = (down_stage, down_work) if which == 0 else (up_stage, up_work)
        return pltpu.make_async_copy(stage.at[g], work.at[g], local_sem.at[2])

    @pl.loop(0, chunks)
    def _(c):
        own_copy(c).start()

    def pick(source, local, stage):
        piece = local.shape[2]

        @pl.loop(0, source.shape[2] // piece)
        def _(p):
            span = pl.ds(pl.multiple_of(p * piece, piece), piece)
            load = pltpu.make_async_copy(source.at[:, :, span], local, local_sem.at[1])
            load.start()
            load.wait()

            @pl.loop(0, groups)
            def _(d):
                for k in range(pair):
                    stage[d, k * rank:(k + 1) * rank, span] = local[pairings[g, k, d]]

    pick(down, down_local, down_stage)
    for k in range(1, groups):
        factor_send(0, k).start()
    factor_own(0).start()
    factor_own(0).wait()
    pick(up, up_local, up_stage)
    for k in range(1, groups):
        factor_send(1, k).start()
    factor_own(1).start()
    factor_own(1).wait()

    @pl.loop(0, tp)
    def _(j):
        weight_copy(j).start()

    @pl.loop(0, chunks)
    def _(c):
        own_copy(c).wait()

    @pl.loop(0, tp)
    def _(j):
        weight_copy(j).wait()

    tile = divisor(columns, 1024)

    def product(j, c, first=False, last=False):
        @pl.loop(0, columns // tile)
        def _(n):
            span = pl.ds(pl.multiple_of(n * tile, tile), tile)
            value = jnp.dot(
                gathered[j * chunks + c], weights[j, features(c), span],
                preferred_element_type=jnp.float32,
            )
            if not first:
                value = acc[:, span] + value
            if last:
                out[:, span] = value.astype(out.dtype)
            else:
                acc[:, span] = value

    product(t, 0, True)

    @pl.loop(1, chunks)
    def _(c):
        product(t, c)

    for i in range(batch // 128):
        row = jnp.broadcast_to(slots[i:i + 1, :], (128, 128))
        slot_lanes[i * 128:(i + 1) * 128, :] = row.T

    for k in range(1, groups):
        factor_send(0, k).wait_recv()
    lane = lax.broadcasted_iota(jnp.int32, (batch, lanes), 1)
    lane_pair = lane // rank

    def one_group(s, total):
        def one_part(c, scores):
            return scores + lax.dot_general(
                gathered[t * chunks + c], down_work[s, :, features(c)], (((1,), (1,)), ((), ())),
                preferred_element_type=jnp.float32,
            )

        scores = lax.fori_loop(0, chunks, one_part, jnp.zeros((batch, lanes), jnp.float32))
        return total + jnp.where(slot_lanes[...] == s * pair + lane_pair, scores, 0.0)

    chosen = lax.fori_loop(0, groups, one_group, jnp.zeros((batch, lanes), jnp.float32))
    folded = chosen + pltpu.roll(chosen, rank, 1)
    low_lane = lax.broadcasted_iota(jnp.int32, (half, lanes), 1) < rank
    own_rank[...] = jnp.where(low_lane, folded[:half], folded[half:])

    def rank_pass(way, to):
        source, target = (low_out, low_in) if way == 0 else (high_out, high_in)
        return pltpu.make_async_remote_copy(
            src_ref=source, dst_ref=target,
            send_sem=rank_send.at[way], recv_sem=rank_recv.at[way],
            device_id={"tp": to}, device_id_type=MESH,
        )

    @pl.when(t == 0)
    def _():
        low_out[...] = own_rank[...]
        rank_pass(0, t + 1).start()

    @pl.when(t == tp - 1)
    def _():
        high_out[...] = own_rank[...]
        rank_pass(1, t - 1).start()

    def sum_pass(to):
        return pltpu.make_async_remote_copy(
            src_ref=sum_out, dst_ref=sum_in,
            send_sem=rank_send.at[2 + jnp.where(t > to, 1, 0)], recv_sem=rank_recv.at[2],
            device_id={"tp": to}, device_id_type=MESH,
        )

    inner = (t > 0) & (t < tp - 1)

    def rank_hop(s):
        @pl.when(inner & (t == s))
        def _():
            rank_pass(0, t).wait_recv()

            @pl.when(t < tp - 2)
            def _():
                low_out[...] = low_in[...] + own_rank[...]
                rank_pass(0, t + 1).start()

        @pl.when(inner & (t == tp - 1 - s))
        def _():
            rank_pass(1, t).wait_recv()

            @pl.when(t > 1)
            def _():
                high_out[...] = high_in[...] + own_rank[...]
                rank_pass(1, t - 1).start()

        @pl.when(inner & (s == tp - 2))
        def _():
            own_rank[...] += low_in[...] + high_in[...]
            sum_out[...] = own_rank[...].astype(sum_out.dtype)

            @pl.when(t == 1)
            def _():
                sum_pass(0).start()

            @pl.when(t == tp - 2)
            def _():
                sum_pass(tp - 1).start()

    def add_adapters():
        @pl.when(jnp.logical_not(inner))
        def _():
            sum_pass(t).wait_recv()
            own_rank[...] = sum_in[...].astype(jnp.float32)

        packed = own_rank[...]
        turned = pltpu.roll(packed, rank, 1)
        sums = jnp.concatenate(
            [jnp.where(low_lane, packed, turned), jnp.where(low_lane, turned, packed)], axis=0
        )
        for k in range(1, groups):
            factor_send(1, k).wait_recv()

        @pl.loop(0, groups)
        def _(s):
            spread = jnp.where(slot_lanes[...] == s * pair + lane_pair, sums, 0.0).astype(jnp.bfloat16)

            @pl.loop(0, columns // tile)
            def _(n):
                span = pl.ds(pl.multiple_of(n * tile, tile), tile)
                acc[:, span] += jnp.dot(
                    spread, up_work[s, :, span], preferred_element_type=jnp.float32
                )

    @pl.loop(1, tp)
    def _(s):
        @pl.loop(0, chunks)
        def _(c):
            @pl.when(t >= s)
            def _():
                passed(t - s, s - 1, c, t, up_send, up_recv).wait_recv()

                @pl.when(t < tp - 1)
                def _():
                    passed(t - s, s, c, t + 1, up_send, up_recv).start()

            @pl.when(t + s < tp)
            def _():
                passed(t + s, s - 1, c, t, dn_send, dn_recv).wait_recv()

                @pl.when(t > 0)
                def _():
                    passed(t + s, s, c, t - 1, dn_send, dn_recv).start()

            @pl.when(c == 0)
            def _():
                rank_hop(s)

                @pl.when(s == tp - 1)
                def _():
                    add_adapters()

            closing = (s == tp - 1) & (c == chunks - 1)

            @pl.when((t >= s) & jnp.logical_not(closing))
            def _():
                product(t - s, c)

            @pl.when((t + s < tp) & jnp.logical_not(closing))
            def _():
                product(t + s, c)

            @pl.when(closing & jnp.logical_not(inner))
            def _():
                product(tp - 1 - t, c, last=True)

            @pl.when(closing & inner)
            def _():
                @pl.loop(0, columns // tile)
                def _(n):
                    span = pl.ds(pl.multiple_of(n * tile, tile), tile)
                    out[:, span] = acc[:, span].astype(out.dtype)

    @pl.loop(0, tp)
    def _(s):
        @pl.loop(0, chunks)
        def _(c):
            @pl.when((t >= s) & (t < tp - 1))
            def _():
                passed(t, s, c, t, up_send, up_recv).wait_send()

            @pl.when((t + s < tp) & (t > 0))
            def _():
                passed(t, s, c, t, dn_send, dn_recv).wait_send()

    @pl.when(t < tp - 2)
    def _():
        rank_pass(0, t).wait_send()

    @pl.when(t > 1)
    def _():
        rank_pass(1, t).wait_send()

    @pl.when(t == 1)
    def _():
        sum_pass(0).wait_send()

    @pl.when(t == tp - 2)
    def _():
        sum_pass(tp - 1).wait_send()

    for which in range(2):
        for k in range(1, groups):
            factor_send(which, k).wait_send()


def body(tp, groups, acts, weight, down, up, pairings, slots):
    batch, depth = acts.shape
    columns = weight.shape[1]
    down = jnp.swapaxes(down, 1, 2)
    pairings = jnp.swapaxes(pairings, 1, 2)
    slots = slots.reshape(batch // 128, 128)
    held, rank, _ = down.shape
    lanes = pairings.shape[1] * rank
    part = divisor(depth, 256)
    chunks = depth // part
    down_piece, up_piece = divisor(depth, 512), divisor(columns, 512)
    bf16, f32 = jnp.bfloat16, jnp.float32
    anywhere = pl.BlockSpec(memory_space=pl.ANY)
    flops = 2 * batch * columns * depth * tp + 2 * batch * groups * lanes * (depth + columns)
    packed = pltpu.VMEM((batch // 2, lanes), f32)
    return pl.pallas_call(
        functools.partial(kernel, tp, groups, chunks),
        out_shape=pltpu.VMEM((batch, columns), bf16),
        in_specs=[anywhere] * 4
        + [pl.BlockSpec(memory_space=pltpu.SMEM), pl.BlockSpec(memory_space=pltpu.VMEM)],
        out_specs=pl.BlockSpec(memory_space=pltpu.VMEM),
        scratch_shapes=[
            pltpu.VMEM((tp * chunks, batch, part), bf16),
            pltpu.VMEM((tp, depth, columns), bf16),
            pltpu.VMEM((batch, columns), f32),
            pltpu.VMEM((held, rank, down_piece), bf16),
            pltpu.VMEM((held, rank, up_piece), bf16),
            pltpu.VMEM((groups, lanes, depth), bf16),
            pltpu.VMEM((groups, lanes, columns), bf16),
            pltpu.VMEM((groups, lanes, depth), bf16),
            pltpu.VMEM((groups, lanes, columns), bf16),
            packed, packed, packed, packed, packed,
            pltpu.VMEM((batch // 2, lanes), bf16),
            pltpu.VMEM((batch // 2, lanes), bf16),
            pltpu.VMEM((batch, lanes), jnp.int32),
            pltpu.SemaphoreType.DMA((tp, chunks)),
            pltpu.SemaphoreType.DMA((tp, chunks)),
            pltpu.SemaphoreType.DMA((tp, chunks)),
            pltpu.SemaphoreType.DMA((tp, chunks)),
            pltpu.SemaphoreType.DMA((2, groups)),
            pltpu.SemaphoreType.DMA((2, groups)),
            pltpu.SemaphoreType.DMA((4,)),
            pltpu.SemaphoreType.DMA((3,)),
            pltpu.SemaphoreType.DMA((tp,)),
            pltpu.SemaphoreType.DMA((chunks,)),
            pltpu.SemaphoreType.DMA((3,)),
        ],
        compiler_params=pltpu.CompilerParams(
            collective_id=0, has_side_effects=True, vmem_limit_bytes=57 << 20
        ),
        cost_estimate=pl.CostEstimate(
            flops=flops, bytes_accessed=2 * (weight.size + 3 * acts.size), transcendentals=0
        ),
    )(acts, weight, down, up, pairings, slots)


def solution(mesh):
    placed = (
        P(("dom", "grp"), "tp"),
        P(None, "tp"),
        P("grp", "tp", None),
        P("grp", None, "tp"),
        P("dom", None, None),
        P(("dom", "grp")),
    )
    return jax.shard_map(
        functools.partial(body, mesh.shape["tp"], mesh.shape["grp"]),
        mesh=mesh, in_specs=placed, out_specs=P(("dom", "grp"), "tp"), check_vma=False,
    )
```
